32 devices in a mesh: fsdp: 16 (over z, x, core), tensor: 2 (over y).
Axes of the slice: x: 2, y: 2, z: 4, core: 2. Of those that a mesh axis runs over, the one named last changes fastest.
Arguments:
- grad: bfloat16 [16384, 8192], P('tensor', 'fsdp'), may hold values from -0.26953125 to 0.26953125
- owner: int32 [4, 8], replicated, may hold values from 0 to 7, each once within a row
- codes: int32 [2, 16384, 8192], P(None, 'tensor', 'fsdp'), may hold values from 0 to 15
- scale_ids: int32 [2, 128, 8192], P(None, 'tensor', 'fsdp'), may hold values from 0 to 15
- scale_table: float32 [16], replicated, may hold values from 0.1 to 1
Outputs:
- statistics: float32 [2, 16384, 8192], P(None, 'tensor', 'fsdp')
The draws below stay inside these ranges and needn't reach their ends.
Inputs may be any that keep to these rules, and one draw needn't show every extreme that they name: Each row owner[c] holds every slot 0 to 7 once: block row r of block column c keeps its statistics at slot owner[c, r].
All inputs are finite; a program needn't handle non-finite values.
Results may differ from the reference program's by a relative error of at most 0.0003.
Values may be sent and summed in bfloat16 or wider, within the bound.
A program may use at most 192 MiB of HBM per device.

```python
import math
import jax
import jax.numpy as jnp
from jax import lax

D = 8192
B = 2048
FF_WIN = 16384
QG = 128
LEVELS = 16
NBR = 8
NCB = 4


def touch_ends(values, key, smallest, largest):
    place = [jax.random.randint(jax.random.fold_in(key, axis), (), 0, length) for axis, length in enumerate(values.shape)]
    longest = values.shape.index(max(values.shape))
    next_to = place[:longest] + [(place[longest] + 1) % values.shape[longest]] + place[longest + 1:]
    return values.at[tuple(place)].set(smallest).at[tuple(next_to)].set(largest)


def steps_of(own_key, extent, cuts, low, largest):
    def one(position, parts):
        heights = jax.random.uniform(jax.random.fold_in(jax.random.fold_in(own_key, 6), position), (parts,), jnp.float32, low / len(cuts), largest / len(cuts))
        return jnp.repeat(jnp.exp(heights), extent[position] // parts).reshape((-1,) + (1,) * (len(extent) - position - 1))

    factor_of = one(*cuts[0])
    for cut in cuts[1:]:
        factor_of = factor_of * one(*cut)
    return factor_of


def centred(stream_key, dims, spread, most, shards=(), held_as=jnp.bfloat16):
    gain = steps_of(stream_key, dims, shards, -0.22, 0.18) if shards else 1.0
    array = jax.random.normal(stream_key, dims, jnp.float32) * spread * gain
    return jnp.minimum(jnp.maximum(array, -most), most).astype(held_as)


def setup_inputs(seed: int = 0) -> dict:
    key_list = jax.random.split(jax.random.key(seed), 6)
    grad = centred(key_list[0], (FF_WIN, D), 0.045, 0.26953125, ((0, 2), (1, 16)))
    owner = jax.vmap(lambda own: jax.random.permutation(own, NBR))(jax.random.split(key_list[1], NCB)).reshape((NCB, NBR)).astype(jnp.int32)
    codes = touch_ends(jax.random.randint(key_list[2], (2, FF_WIN, D), 0, 16), jax.random.fold_in(key_list[2], 1), 0, 15).astype(jnp.int32)
    scale_ids = touch_ends(jax.random.randint(key_list[3], (2, FF_WIN // QG, D), 0, LEVELS), jax.random.fold_in(key_list[3], 1), 0, LEVELS - 1).astype(jnp.int32)
    scale_table = jnp.clip(jnp.exp(jax.random.uniform(key_list[4], (LEVELS,), jnp.float32, math.log(0.1), math.log(1.0))), 0.1, 1.0)
    return {"grad": grad, "owner": owner, "codes": codes, "scale_ids": scale_ids, "scale_table": scale_table}


def gram_pair(single_block):
    left_gram = jnp.dot(single_block, single_block.T, precision=lax.Precision.HIGHEST)
    right_gram = jnp.dot(single_block.T, single_block, precision=lax.Precision.HIGHEST)
    return jnp.stack([left_gram, right_gram])


def reference(grad, owner, codes, scale_ids, scale_table):
    slot_rows = jnp.argsort(owner, axis=1).astype(jnp.int32)
    blocks = grad.astype(jnp.float32).reshape(NBR, B, NCB, B).transpose(2, 0, 1, 3)
    placed = jax.vmap(lambda column_blocks, order_row: column_blocks[order_row])(blocks, slot_rows)
    flat_blocks = placed.reshape(NCB * NBR, B, B)
    result = lax.map(gram_pair, flat_blocks).reshape(NCB, NBR, 2, B, B)
    stacked = result.transpose(2, 1, 3, 0, 4).reshape(2, NBR * B, NCB * B)
    scale_grid = jnp.repeat(scale_table[scale_ids], QG, axis=1)
    previous = scale_grid * ((codes.astype(jnp.float32) - 7.5) / 7.5)
    return 0.9 * previous + 0.1 * stacked
```

```python
import functools

import jax
import jax.numpy as jnp
from jax import lax
from jax.experimental import pallas as pl
from jax.experimental.pallas import tpu as pltpu
from jax.sharding import PartitionSpec as P

B = 2048


def partner_2(value, axis, bit):
    mask = 2**bit
    pairs = [(source, source ^ mask) for source in range(lax.axis_size(axis))]
    return lax.ppermute(value, axis, pairs)


def left_part(slab_piece, member, piece_width):
    own_rows = lax.dynamic_slice_in_dim(slab_piece, member * piece_width, piece_width, 1)
    return jnp.einsum("sbj,scj->sbc", slab_piece, own_rows, preferred_element_type=jnp.float32)


def right_part(slab_piece, own_piece):
    return jnp.einsum("sbj,sbc->sjc", slab_piece, own_piece, preferred_element_type=jnp.float32)


def general_shards(grad, owner, codes, scale_ids, scale_table):
    rows_here = grad.shape[0]
    width_here = grad.shape[1]
    slot_count = rows_here // B
    tensor_count = lax.axis_size("tensor")
    group_size = B // width_here
    tensor_pos = lax.axis_index("tensor")
    fsdp_pos = lax.axis_index("fsdp")
    column_block = fsdp_pos // group_size
    member = fsdp_pos % group_size
    owner_row = lax.dynamic_index_in_dim(owner, column_block, 0, keepdims=False)
    pieces = grad.reshape(slot_count, B, width_here)
    local_slots = lax.dynamic_slice_in_dim(owner_row, tensor_pos * slot_count, slot_count)
    targets = jnp.arange(tensor_count * slot_count, dtype=jnp.int32).reshape(
        tensor_count, slot_count
    )
    select = (targets[:, :, None] == local_slots[None, None, :]).astype(jnp.bfloat16)
    outgoing = jnp.einsum(
        "dsr,rbc->dsbc", select, pieces, preferred_element_type=jnp.float32
    ).astype(jnp.bfloat16)
    incoming = lax.all_to_all(outgoing, "tensor", split_axis=0, concat_axis=0, tiled=True)
    owned_block = jnp.sum(incoming, axis=0, dtype=jnp.float32).astype(jnp.bfloat16)
    depth_count = group_size.bit_length() - 1
    collected = owned_block
    for step_bit in range(depth_count):
        partner = partner_2(collected, "fsdp", step_bit)
        upper_half = fsdp_pos // (1 << step_bit) % 2 == 1
        collected = jnp.where(
            upper_half,
            jnp.concatenate([partner, collected], 2),
            jnp.concatenate([collected, partner], 2),
        )
    left_gram = left_part(collected, member, width_here)
    right_gram = right_part(collected, owned_block)
    stacked = jnp.stack(
        [left_gram.reshape(rows_here, width_here), right_gram.reshape(rows_here, width_here)]
    )
    group_rows = rows_here // scale_ids.shape[1]
    level_index = jnp.arange(scale_table.shape[0], dtype=jnp.int32)
    scale_grid = jnp.sum(jnp.where(scale_ids[..., None] == level_index, scale_table, 0.0), axis=-1)
    previous = scale_grid[:, :, None, :] * (
        (codes.reshape(2, -1, group_rows, width_here).astype(jnp.float32) - 7.5) / 7.5
    )
    previous = previous.reshape(2, rows_here, width_here)
    return 0.9 * previous + 0.1 * stacked


def fold_kernel(levels, group_rows, aliased, place, table, *refs):
    piece_refs = refs[:4]
    codes, ids = refs[4:6]
    out, scales = refs[-2:]
    width = codes.shape[2]
    half, tile = pl.program_id(0), pl.program_id(1)
    member = place[1]

    @pl.when(tile == 0)
    def _():
        wanted = ids[0]
        found = jnp.zeros(wanted.shape, jnp.float32)
        for level in range(levels):
            found = jnp.where(wanted == level, table[level], found)
        scales[...] = found * (0.9 / 7.5)

    def blend(gram, out_tile):
        for group in range(width // group_rows):
            rows = pl.ds(group * group_rows, group_rows)
            scale = scales[pl.ds(out_tile * (width // group_rows) + group, 1), :]
            stored = scale * (codes[0, rows, :].astype(jnp.float32) - 7.5)
            out[0, rows, :] = stored + 0.1 * gram[group * group_rows : (group + 1) * group_rows]

    @pl.when(half == 0)
    def _():
        here = pl.ds(pl.multiple_of(tile * width, width), width)
        own = pl.ds(pl.multiple_of(member * width, width), width)
        gram = None
        for piece in piece_refs:
            term = lax.dot_general(
                piece[here, :],
                piece[own, :],
                (((1,), (1,)), ((), ())),
                preferred_element_type=jnp.float32,
            )
            gram = term if gram is None else gram + term
        blend(gram, tile)

    for position, piece in enumerate(piece_refs):

        @pl.when((half == 1) & (tile == position))
        def _():
            gram = lax.dot_general(
                piece[...],
                piece_refs[0][...],
                (((0,), (0,)), ((), ())),
                preferred_element_type=jnp.float32,
            )
            blend(gram, lax.bitwise_xor(member, position))


def fold(place, scale_table, pieces, codes, scale_ids, filled):
    width = codes.shape[2]
    tiles = B // width
    id_rows = scale_ids.shape[1] // (codes.shape[1] // B)
    group_rows = B // id_rows

    def tile_of(half, tile, place, table):
        placed = jnp.where(half == 0, tile, lax.bitwise_xor(place[1], tile))
        return half, place[0] * tiles + placed, 0

    def whole(half, tile, place, table):
        return 0, 0

    in_specs = [pl.BlockSpec((B, width), whole, pipeline_mode=pl.Buffered(1))] * len(pieces)
    in_specs.append(pl.BlockSpec((1, width, width), tile_of))
    in_specs.append(
        pl.BlockSpec((1, id_rows, width), lambda half, tile, place, table: (half, place[0], 0))
    )
    operands = [place, scale_table, *pieces, codes, scale_ids]
    aliases = {}
    if filled is not None:
        in_specs.append(pl.BlockSpec(memory_space=pl.ANY))
        aliases = {len(operands): 0}
        operands.append(filled)
    return pl.pallas_call(
        functools.partial(
            fold_kernel, scale_table.shape[0], group_rows, filled is not None
        ),
        out_shape=jax.ShapeDtypeStruct(codes.shape, jnp.float32),
        grid_spec=pltpu.PrefetchScalarGridSpec(
            num_scalar_prefetch=2,
            grid=(2, tiles),
            in_specs=in_specs,
            out_specs=pl.BlockSpec((1, width, width), tile_of),
            scratch_shapes=[pltpu.VMEM((id_rows, width), jnp.float32)],
        ),
        input_output_aliases=aliases,
        compiler_params=pltpu.CompilerParams(vmem_limit_bytes=40 * 2**20),
        cost_estimate=pl.CostEstimate(
            flops=4 * B * B * width, bytes_accessed=5 * 2 * B * width * 4, transcendentals=0
        ),
        name="fold",
    )(*operands)


def shards(grad, owner, codes, scale_ids, scale_table):
    width = grad.shape[1]
    slot_count = grad.shape[0] // B
    group_size = B // width
    tensor_pos = lax.axis_index("tensor")
    fsdp_pos = lax.axis_index("fsdp")
    member = fsdp_pos % group_size
    column = fsdp_pos // group_size
    pieces = grad.reshape(slot_count, B, width)

    by_home = owner.reshape(-1, 2, slot_count)
    home = jnp.arange(2, dtype=jnp.int32)[None, :, None]
    leaves = (by_home // slot_count != home).astype(jnp.int32)
    order = jnp.argsort(leaves, axis=2, stable=True).astype(jnp.int32)
    leaving = jnp.sum(leaves, axis=2)[:, 0]
    most_leaving = jnp.max(leaving)
    my_order = order[column, tensor_pos]
    staying = slot_count - leaving[column]
    source = jnp.where(jnp.arange(slot_count) < staying, tensor_pos, 1 - tensor_pos)
    my_slots = by_home[column, source, order[column, source, jnp.arange(slot_count)]] % slot_count

    def cross(value):
        return partner_2(value, "tensor", 0)

    def taken(step):
        return lax.dynamic_index_in_dim(pieces, my_order[step], 0, keepdims=False)

    first = lax.cond(most_leaving == slot_count, cross, lambda value: value, taken(0))
    blocks = [jnp.where(staying > 0, taken(0), first)]
    received = None
    for step in range(1, slot_count):
        sent = taken(step)
        if received is not None:
            sent, received = lax.optimization_barrier((sent, received))
        received = cross(sent)
        blocks.append(jnp.where(step < staying, sent, received))
    results = []
    for step, own in enumerate(blocks):
        if step >= 2:
            own, results[step - 2] = lax.optimization_barrier((own, results[step - 2]))
        across = partner_2(own, "fsdp", 1)
        beside = partner_2(own, "fsdp", 0)
        diagonal = partner_2(across, "fsdp", 0)
        place = jnp.stack([my_slots[step], member]).astype(jnp.int32)
        filled = results[step - 1] if step > 0 else None
        results.append(
            fold(place, scale_table, [own, beside, across, diagonal], codes, scale_ids, filled)
        )
    return results[-1]


def solution(mesh):
    in_specs = (P("tensor", "fsdp"), P(), P(None, "tensor", "fsdp"), P(None, "tensor", "fsdp"), P())
    out_specs = P(None, "tensor", "fsdp")

    def update(grad, owner, codes, scale_ids, scale_table):
        width = grad.shape[1] // mesh.shape["fsdp"]
        fits = mesh.shape["tensor"] == 2 and width * 4 == B
        body = shards if fits else general_shards
        return jax.shard_map(
            body, mesh=mesh, in_specs=in_specs, out_specs=out_specs, check_vma=False
        )(grad, owner, codes, scale_ids, scale_table)

    return update
```

```python
import functools

import jax
import jax.numpy as jnp
from jax import lax
from jax.experimental import pallas as pl
from jax.experimental.pallas import tpu as pltpu
from jax.sharding import PartitionSpec as P

B = 2048


def partner_2(value, axis, bit):
    mask = 2**bit
    pairs = [(source, source ^ mask) for source in range(lax.axis_size(axis))]
    return lax.ppermute(value, axis, pairs)


def left_part(slab_piece, member, piece_width):
    own_rows = lax.dynamic_slice_in_dim(slab_piece, member * piece_width, piece_width, 1)
    return jnp.einsum("sbj,scj->sbc", slab_piece, own_rows, preferred_element_type=jnp.float32)


def right_part(slab_piece, own_piece):
    return jnp.einsum("sbj,sbc->sjc", slab_piece, own_piece, preferred_element_type=jnp.float32)


def general_shards(grad, owner, codes, scale_ids, scale_table):
    rows_here = grad.shape[0]
    width_here = grad.shape[1]
    slot_count = rows_here // B
    tensor_count = lax.axis_size("tensor")
    group_size = B // width_here
    tensor_pos = lax.axis_index("tensor")
    fsdp_pos = lax.axis_index("fsdp")
    column_block = fsdp_pos // group_size
    member = fsdp_pos % group_size
    owner_row = lax.dynamic_index_in_dim(owner, column_block, 0, keepdims=False)
    pieces = grad.reshape(slot_count, B, width_here)
    local_slots = lax.dynamic_slice_in_dim(owner_row, tensor_pos * slot_count, slot_count)
    targets = jnp.arange(tensor_count * slot_count, dtype=jnp.int32).reshape(
        tensor_count, slot_count
    )
    select = (targets[:, :, None] == local_slots[None, None, :]).astype(jnp.bfloat16)
    outgoing = jnp.einsum(
        "dsr,rbc->dsbc", select, pieces, preferred_element_type=jnp.float32
    ).astype(jnp.bfloat16)
    incoming = lax.all_to_all(outgoing, "tensor", split_axis=0, concat_axis=0, tiled=True)
    owned_block = jnp.sum(incoming, axis=0, dtype=jnp.float32).astype(jnp.bfloat16)
    depth_count = group_size.bit_length() - 1
    collected = owned_block
    for step_bit in range(depth_count):
        partner = partner_2(collected, "fsdp", step_bit)
        upper_half = fsdp_pos // (1 << step_bit) % 2 == 1
        collected = jnp.where(
            upper_half,
            jnp.concatenate([partner, collected], 2),
            jnp.concatenate([collected, partner], 2),
        )
    left_gram = left_part(collected, member, width_here)
    right_gram = right_part(collected, owned_block)
    stacked = jnp.stack(
        [left_gram.reshape(rows_here, width_here), right_gram.reshape(rows_here, width_here)]
    )
    group_rows = rows_here // scale_ids.shape[1]
    level_index = jnp.arange(scale_table.shape[0], dtype=jnp.int32)
    scale_grid = jnp.sum(jnp.where(scale_ids[..., None] == level_index, scale_table, 0.0), axis=-1)
    previous = scale_grid[:, :, None, :] * (
        (codes.reshape(2, -1, group_rows, width_here).astype(jnp.float32) - 7.5) / 7.5
    )
    previous = previous.reshape(2, rows_here, width_here)
    return 0.9 * previous + 0.1 * stacked


def plan_kernel(slot_count, group_size, owner, plan):
    tensor_pos = lax.axis_index("tensor")
    fsdp_pos = lax.axis_index("fsdp")
    column = lax.div(fsdp_pos, group_size)
    columns = owner.shape[0]

    def stays(block_column, block_row, home):
        slot = owner[block_column, block_row]
        return ((slot >= slot_count).astype(jnp.int32) == home).astype(jnp.int32)

    all_leave = jnp.int32(0)
    for block_column in range(columns):
        kept = sum(stays(block_column, row, 0) for row in range(slot_count))
        all_leave = jnp.maximum(all_leave, (kept == 0).astype(jnp.int32))
    first_row = tensor_pos * slot_count
    staying = sum(stays(column, first_row + row, tensor_pos) for row in range(slot_count))
    keep_at, leave_at = jnp.int32(0), staying
    for row in range(slot_count):
        kept = stays(column, first_row + row, tensor_pos)
        place = jnp.where(kept == 1, keep_at, leave_at)
        plan[place] = jnp.int32(row)

        @pl.when(kept == 1)
        def _():
            plan[slot_count + place] = owner[column, first_row + row] - first_row

        keep_at, leave_at = keep_at + kept, leave_at + 1 - kept
    arrive_at = staying
    other_row = slot_count - first_row
    for row in range(slot_count):
        comes = stays(column, other_row + row, tensor_pos)

        @pl.when(comes == 1)
        def _():
            plan[slot_count + arrive_at] = owner[column, other_row + row] - first_row

        arrive_at = arrive_at + comes
    plan[2 * slot_count] = staying
    plan[2 * slot_count + 1] = all_leave
    plan[2 * slot_count + 2] = lax.rem(fsdp_pos, group_size)
    plan[2 * slot_count + 3] = jnp.int32(0)


def make_plan(owner, slot_count, group_size):
    return pl.pallas_call(
        functools.partial(plan_kernel, slot_count, group_size),
        out_shape=jax.ShapeDtypeStruct((2 * slot_count + 4,), jnp.int32),
        in_specs=[pl.BlockSpec(memory_space=pltpu.SMEM)],
        out_specs=pl.BlockSpec(memory_space=pltpu.SMEM),
        name="plan",
    )(owner)


def fold_kernel(levels, group_rows, slot_count, positions, cuts, plan, table, *refs):
    count = len(positions)
    adds = positions[0] != 0
    piece_refs = [refs[i * cuts : (i + 1) * cuts] for i in range(count)]
    own_refs = refs[count * cuts : (count + 1) * cuts] if adds else piece_refs[0]
    codes, ids = refs[(count + adds) * cuts : (count + adds) * cuts + 2]
    filled = refs[-3]
    out, strips = refs[-2:]
    width = codes.shape[2]
    tiles = B // width
    chunk_tiles = tiles // cuts
    item = pl.program_id(0)
    member = plan[2 * slot_count + 2]
    member_chunk = lax.div(member, chunk_tiles)
    member_rows = pl.ds(pl.multiple_of(lax.rem(member, chunk_tiles) * width, width), width)

    for cut in range(cuts):

        @pl.when((item == 0) & (member_chunk == cut))
        def _():
            for place, piece in enumerate(piece_refs):
                strips[place] = piece[cut][member_rows, :]

    def blend(gram, out_tile):
        wanted = ids[0, pl.ds(0, ids.shape[1]), :]
        found = jnp.zeros(wanted.shape, jnp.float32)
        for level in range(levels):
            found = jnp.where(wanted == level, table[level], found)
        found = found * (0.9 / 7.5)
        groups = width // group_rows
        for tile in range(tiles):

            @pl.when(out_tile == tile)
            def _():
                for group in range(groups):
                    rows = pl.ds(group * group_rows, group_rows)
                    line = tile * groups + group
                    stored = found[line : line + 1] * (codes[0, rows, :].astype(jnp.float32) - 7.5)
                    out[0, rows, :] = (
                        stored + 0.1 * gram[group * group_rows : (group + 1) * group_rows]
                    )

    for cut in range(cuts):

        @pl.when((item >= cut * chunk_tiles) & (item < (cut + 1) * chunk_tiles))
        def _():
            first = pl.multiple_of((item - cut * chunk_tiles) * width, width)
            gram = None
            for place, piece in enumerate(piece_refs):
                term = lax.dot_general(
                    piece[cut][pl.ds(first, width), :],
                    strips[place],
                    (((1,), (1,)), ((), ())),
                    preferred_element_type=jnp.float32,
                )
                gram = term if gram is None else gram + term
            if adds:
                out[0] = filled[0] + 0.1 * gram
            else:
                blend(gram, item)

    for place, piece in enumerate(piece_refs):

        @pl.when(item == tiles + place)
        def _():
            gram = None
            for cut in range(cuts):
                term = lax.dot_general(
                    piece[cut][...],
                    own_refs[cut][...],
                    (((0,), (0,)), ((), ())),
                    preferred_element_type=jnp.float32,
                )
                gram = term if gram is None else gram + term
            blend(gram, lax.bitwise_xor(member, positions[place]))


def fold(step, plan, scale_table, positions, pieces, codes, scale_ids, filled):
    width = codes.shape[2]
    tiles = B // width
    slot_count = codes.shape[1] // B
    id_rows = scale_ids.shape[1] // slot_count
    cuts = len(pieces[0])
    adds = positions[0] != 0

    def tile_of(item, plan, table):
        right = item >= tiles
        placed = jnp.where(right, plan[2 * slot_count + 2] ^ (item - tiles + positions[0]), item)
        return right.astype(jnp.int32), plan[slot_count + step] * tiles + placed, 0

    def code_of(item, plan, table):
        return tile_of(jnp.maximum(item, tiles) if adds else item, plan, table)

    def filled_of(item, plan, table):
        return tile_of(jnp.minimum(item, tiles - 1), plan, table)

    def ids_of(item, plan, table):
        right = jnp.maximum(item, tiles) >= tiles if adds else item >= tiles
        return right.astype(jnp.int32), plan[slot_count + step], 0

    operands = [plan, scale_table]
    in_specs = []
    for piece in pieces:
        for chunk in piece:
            in_specs.append(
                pl.BlockSpec(chunk.shape, lambda *_: (0, 0), pipeline_mode=pl.Buffered(1))
            )
            operands.append(chunk)
    in_specs.append(pl.BlockSpec((1, width, width), code_of))
    in_specs.append(pl.BlockSpec((1, id_rows, width), ids_of))
    operands += [codes, scale_ids]
    aliases = {}
    if filled is not None:
        if adds:
            in_specs.append(pl.BlockSpec((1, width, width), filled_of))
        else:
            in_specs.append(pl.BlockSpec(memory_space=pl.ANY))
        aliases = {len(operands): 0}
        operands.append(filled)
    count = len(positions)
    return pl.pallas_call(
        functools.partial(
            fold_kernel, scale_table.shape[0], B // id_rows, slot_count, positions, cuts
        ),
        out_shape=jax.ShapeDtypeStruct(codes.shape, jnp.float32),
        grid_spec=pltpu.PrefetchScalarGridSpec(
            num_scalar_prefetch=2,
            grid=(tiles + count,),
            in_specs=in_specs,
            out_specs=pl.BlockSpec((1, width, width), tile_of),
            scratch_shapes=[pltpu.VMEM((count, width, width), jnp.bfloat16)],
        ),
        input_output_aliases=aliases,
        compiler_params=pltpu.CompilerParams(vmem_limit_bytes=40 * 2**20),
        cost_estimate=pl.CostEstimate(
            flops=B * B * width * count,
            bytes_accessed=(tiles + count) * width * width * 8,
            transcendentals=0,
        ),
        name="fold",
    )(*operands)


CUTS = 2


def shards(grad, owner, codes, scale_ids, scale_table):
    width = grad.shape[1]
    slot_count = grad.shape[0] // B
    chunk_rows = B // CUTS
    plan = make_plan(owner, slot_count, B // width)
    staying = plan[2 * slot_count]

    def cross(value):
        return partner_2(value, "tensor", 0)

    def taken(index, cut):
        return lax.dynamic_slice_in_dim(grad, index * B + cut * chunk_rows, chunk_rows, 0)

    def exchanged(index):
        chunks = [taken(index, cut) for cut in range(CUTS)]
        return [jnp.where(staying > 0, chunk, cross(chunk)) for chunk in chunks]

    def kept(index):
        return [taken(index, cut) for cut in range(CUTS)]

    blocks = [lax.cond(plan[2 * slot_count + 1] == 1, exchanged, kept, plan[0])]
    arrived = []
    for step in range(1, slot_count):
        block = []
        for cut in range(CUTS):
            index = plan[step]
            if len(arrived) >= 2:
                index, arrived[-2] = lax.optimization_barrier((index, arrived[-2]))
            sent = taken(index, cut)
            arrived.append(cross(sent))
            block.append((sent, len(arrived) - 1))
        blocks.append(block)
    result = None
    for step, block in enumerate(blocks):
        if step == 0:
            own = list(block)
        else:
            own = [jnp.where(step < staying, sent, arrived[place]) for sent, place in block]
        last = step == slot_count - 1
        across = [partner_2(chunk, "fsdp", 1) for chunk in own]
        beside = [partner_2(chunk, "fsdp", 0) for chunk in own]
        if result is not None:
            across[0], result = lax.optimization_barrier((across[0], result))
        if last:
            result = fold(
                step, plan, scale_table, (0, 1), [own, beside], codes, scale_ids, result
            )
            across[-1], result = lax.optimization_barrier((across[-1], result))
        diagonal = [partner_2(chunk, "fsdp", 0) for chunk in across]
        if last:
            positions, pieces = (2, 3), [across, diagonal, own]
        else:
            positions, pieces = (0, 1, 2, 3), [own, beside, across, diagonal]
        result = fold(step, plan, scale_table, positions, pieces, codes, scale_ids, result)
    return result


def solution(mesh):
    in_specs = (P("tensor", "fsdp"), P(), P(None, "tensor", "fsdp"), P(None, "tensor", "fsdp"), P())
    out_specs = P(None, "tensor", "fsdp")

    def update(grad, owner, codes, scale_ids, scale_table):
        width = grad.shape[1] // mesh.shape["fsdp"]
        fits = mesh.shape["tensor"] == 2 and width * 4 == B
        body = shards if fits else general_shards
        return jax.shard_map(
            body, mesh=mesh, in_specs=in_specs, out_specs=out_specs, check_vma=False
        )(grad, owner, codes, scale_ids, scale_table)

    return update
```
